32 devices in a mesh: dp: 8 (over z, y), group: 4 (over x, core).
Axes of the slice: x: 2, y: 2, z: 4, core: 2. Of those that a mesh axis runs over, the one named last changes fastest.
Arguments:
- params: float32 [1774080], P('group'), as said below
- moment1: float32 [1774080], P('group'), may hold values from -0.3 to 0.3
- moment2: float32 [1774080], P('group'), may hold values from 0.0001 to 0.01
- image_in: bfloat16 [64, 197, 384], P(('dp', 'group'))
- cotangent: bfloat16 [64, 197, 384], P(('dp', 'group')), may hold values from -6 to 6
- image_counts: int32 [32], P(('dp', 'group')), may hold values from 1 to 2, as said below
Outputs:
- block_out: bfloat16 [64, 197, 384], P(('dp', 'group'))
- input_grad: bfloat16 [64, 197, 384], P(('dp', 'group'))
- param_grad: float32 [1774080], P('group')
- new_params: float32 [1774080], P('group')
- new_moment1: float32 [1774080], P('group')
- new_moment2: float32 [1774080], P('group')
The draws below stay inside these ranges and needn't reach their ends.
Inputs may be any that keep to these rules, and one draw needn't show every extreme that they name: image_counts gives each device the number of its slots, taken from the first, that hold live images; some device has 2 and some device has 1. params is laid out as in the reference program.
All inputs are finite; a program needn't handle non-finite values.
Results may differ from the reference program's by a relative error of at most 0.0095.
The reference program's roundings to bfloat16 on the way count: a program that leaves them out, or rounds other values in their place, can miss the bound.
Values sent between devices are 32-bit elements; how exact they have to be, the bound alone decides.
A program may use at most 128 MiB of HBM per device.

```python
import math
import jax
import jax.numpy as jnp
from jax import lax

D = 384
HEADS = 6
HEAD_DIM = 64
FF = 1536
S = 197
SLOTS = 2
STEP = 5
RANKS = 32
IMAGES = 64
PARAMS = 1774080


def draw_params(key, part):
    key_list = jax.random.split(key, 1)
    base = jax.random.normal(key_list[0], (PARAMS,), jnp.float32)
    segments = [(D, 0.1, 1.0), (D, 0.3, 0.0), (3 * D * D, D ** (-0.5), 0.0), (D, 0.3, 0.0), (D, 0.3, 0.0), (D * D, 4.0 * D ** (-0.5), 0.0), (D, 0.3, 0.0), (D, 0.1, 1.0), (D, 0.3, 0.0), (D * FF, D ** (-0.5), 0.0), (FF, 0.3, 0.0), (FF * D, FF ** (-0.5), 0.0), (D, 0.3, 0.0)]
    scale_vec = jnp.concatenate([jnp.full((length_one,), scale_one, jnp.float32) for length_one, scale_one, centre_one in segments])
    centre_vec = jnp.concatenate([jnp.full((length_one,), centre_one, jnp.float32) for length_one, scale_one, centre_one in segments])
    values = base * scale_vec + centre_vec
    return values


def draw_image_in(key, part):
    key_list = jax.random.split(key, 2)
    base = jax.random.normal(key_list[0], (IMAGES, S, D), jnp.float32)
    row_scale = 0.4 * jnp.exp(jax.random.uniform(key_list[1], (IMAGES, S, 1), jnp.float32, 0.0, math.log(10.0)))
    values = base * row_scale
    return values.astype(jnp.bfloat16)


def draw_image_counts(key, part):
    order = jax.random.permutation(jax.random.fold_in(key, 11), RANKS)
    counts = jax.random.randint(jax.random.fold_in(key, 12), (RANKS,), 1, SLOTS + 1).astype(jnp.int32)
    counts = counts.at[order[0]].set(SLOTS)
    counts = counts.at[order[1]].set(1)
    return counts


def level_of(key, extent, cuts, least, largest):
    factor_of = 1.0
    for axis_at, shards_of in cuts:
        steps = jax.random.uniform(jax.random.fold_in(jax.random.fold_in(key, 6), axis_at), (shards_of,), jnp.float32, least / len(cuts), largest / len(cuts))
        factor_of = factor_of * jnp.repeat(jnp.exp(steps), extent[axis_at] // shards_of).reshape((-1,) + (1,) * (len(extent) - 1 - axis_at))
    return factor_of


def gaussian(key, dims, scale, reach, cuts=(), kind=jnp.bfloat16):
    drawn = scale * jax.random.normal(key, dims, jnp.float32)
    if cuts:
        drawn = drawn * level_of(key, dims, cuts, -0.22, 0.18)
    return jnp.clip(drawn, -reach, reach).astype(kind)


def setup_inputs(seed: int = 0) -> dict:
    arg_keys = jax.random.split(jax.random.key(seed), 7)
    params = draw_params(jax.random.fold_in(arg_keys[6], 71), 0)
    moment1 = gaussian(arg_keys[1], (PARAMS,), 0.05, 0.3, ((0, 4),), jnp.float32)
    moment2 = jnp.clip(jnp.exp(math.log(0.01) - 4.6051702 * jax.random.uniform(arg_keys[2], (PARAMS,), jnp.float32) ** level_of(arg_keys[2], (PARAMS,), ((0, 4),), -0.2, 0.2)), 0.0001, 0.01)
    image_in = draw_image_in(jax.random.fold_in(arg_keys[6], 71), 0)
    cotangent = gaussian(arg_keys[4], (IMAGES, S, D), 1.0, 6.0, ((0, 32),))
    image_counts = draw_image_counts(jax.random.fold_in(arg_keys[6], 71), 0)
    return {"params": params, "moment1": moment1, "moment2": moment2, "image_in": image_in, "cotangent": cotangent, "image_counts": image_counts}


def unpack(flat_params):
    shapes_all = [(D,), (D,), (D, 3 * D), (D,), (D,), (D, D), (D,), (D,), (D,), (D, FF), (FF,), (FF, D), (D,)]
    offset = 0
    pieces = []
    for shape_one in shapes_all:
        count_one = math.prod(shape_one)
        pieces.append(flat_params[offset:offset + count_one].reshape(shape_one))
        offset = offset + count_one
    return pieces

def layer_norm(values, gain_vec, shift_vec):
    middle = lax.optimization_barrier(jnp.mean(values, axis=-1, keepdims=True))
    spread = lax.optimization_barrier(jnp.mean(jnp.square(values - middle), axis=-1, keepdims=True))
    scaled = lax.rsqrt(spread + 1e-06)
    unit_rows = (values - middle) * scaled
    return (unit_rows * gain_vec + shift_vec, unit_rows, scaled)

def norm_back(upstream, unit_rows, scaled, gain_vec):
    grad_gain = lax.optimization_barrier(jnp.sum(upstream * unit_rows, axis=0))
    grad_shift = lax.optimization_barrier(jnp.sum(upstream, axis=0))
    inner_grad = upstream * gain_vec
    result = scaled * (inner_grad - lax.optimization_barrier(jnp.mean(inner_grad, axis=-1, keepdims=True)) - unit_rows * lax.optimization_barrier(jnp.mean(inner_grad * unit_rows, axis=-1, keepdims=True)))
    return (result, grad_gain, grad_shift)

def block_pass(flat_params, images, upstream, live_rows):
    first_gain, first_shift, input_weight, query_bias, value_bias, output_weight, output_bias, second_gain, second_shift, upward_weight, upward_bias, downward_weight, downward_bias = unpack(flat_params)
    low = jnp.bfloat16
    input_low = input_weight.astype(low)
    output_low = output_weight.astype(low)
    upward_low = upward_weight.astype(low)
    downward_low = downward_weight.astype(low)
    batch_size = images.shape[0]
    row_count = batch_size * S
    inputs = images.reshape(row_count, D).astype(jnp.float32)
    normed_a, unit_a, scale_a = layer_norm(inputs, first_gain, first_shift)
    normed_low = normed_a.astype(low)
    project = jnp.dot(normed_low, input_low, preferred_element_type=jnp.float32)
    head_shape = (batch_size, S, HEADS, HEAD_DIM)
    query_rows = (project[:, :D] + query_bias).astype(low).reshape(head_shape)
    key_rows = project[:, D:2 * D].astype(low).reshape(head_shape)
    value_rows = (project[:, 2 * D:] + value_bias).astype(low).reshape(head_shape)
    factor = HEAD_DIM ** (-0.5)
    scores = jnp.einsum('bqhd,bkhd->bhqk', query_rows.astype(jnp.float32), key_rows.astype(jnp.float32)) * factor
    row_max = lax.optimization_barrier(jnp.max(scores, axis=-1, keepdims=True))
    log_total = row_max + jnp.log(lax.optimization_barrier(jnp.sum(jnp.exp(scores - row_max), axis=-1, keepdims=True)))
    soft_probs = jnp.exp(scores - log_total)
    probs_low = soft_probs.astype(low)
    mixed_rows = jnp.einsum('bhqk,bkhd->bqhd', probs_low.astype(jnp.float32), value_rows.astype(jnp.float32))
    mixed_low = mixed_rows.astype(low).reshape(row_count, D)
    residual = inputs + jnp.dot(mixed_low, output_low, preferred_element_type=jnp.float32) + output_bias
    normed_b, unit_b, scale_b = layer_norm(residual, second_gain, second_shift)
    hidden_in = normed_b.astype(low)
    pre_act = jnp.dot(hidden_in, upward_low, preferred_element_type=jnp.float32) + upward_bias
    activated = jax.nn.gelu(pre_act, approximate=False).astype(low)
    final_rows = residual + jnp.dot(activated, downward_low, preferred_element_type=jnp.float32) + downward_bias
    outputs = (final_rows * live_rows).astype(low).reshape(batch_size, S, D)
    grad_out = upstream.reshape(row_count, D).astype(jnp.float32) * live_rows
    grad_low = grad_out.astype(low)
    grad_down = jnp.dot(activated.T, grad_low, preferred_element_type=jnp.float32)
    grad_down_bias = lax.optimization_barrier(jnp.sum(grad_out, axis=0))
    grad_act = jnp.dot(grad_low, downward_low.T, preferred_element_type=jnp.float32)
    normal_cdf = 0.5 * (1.0 + jax.scipy.special.erf(pre_act * (1.0 / math.sqrt(2.0))))
    density = jnp.exp(-0.5 * pre_act * pre_act) * (1.0 / math.sqrt(2.0 * math.pi))
    grad_pre = grad_act * (normal_cdf + pre_act * density)
    grad_pre_low = grad_pre.astype(low)
    grad_up = jnp.dot(hidden_in.T, grad_pre_low, preferred_element_type=jnp.float32)
    grad_up_bias = lax.optimization_barrier(jnp.sum(grad_pre, axis=0))
    grad_hidden = jnp.dot(grad_pre_low, upward_low.T, preferred_element_type=jnp.float32)
    back_b, grad_gain_b, grad_shift_b = norm_back(grad_hidden, unit_b, scale_b, second_gain)
    grad_resid = grad_out + back_b
    grad_resid_low = grad_resid.astype(low)
    grad_output_w = jnp.dot(mixed_low.T, grad_resid_low, preferred_element_type=jnp.float32)
    grad_output_bias = lax.optimization_barrier(jnp.sum(grad_resid, axis=0))
    grad_mixed = jnp.dot(grad_resid_low, output_low.T, preferred_element_type=jnp.float32).astype(low).reshape(head_shape)
    grad_probs = jnp.einsum('bqhd,bkhd->bhqk', grad_mixed.astype(jnp.float32), value_rows.astype(jnp.float32))
    grad_values = jnp.einsum('bhqk,bqhd->bkhd', probs_low.astype(jnp.float32), grad_mixed.astype(jnp.float32))
    centre = lax.optimization_barrier(jnp.sum(grad_probs * soft_probs, axis=-1, keepdims=True))
    grad_scores = (soft_probs * (grad_probs - centre) * factor).astype(low)
    grad_queries = jnp.einsum('bhqk,bkhd->bqhd', grad_scores.astype(jnp.float32), key_rows.astype(jnp.float32))
    grad_keys = jnp.einsum('bhqk,bqhd->bkhd', grad_scores.astype(jnp.float32), query_rows.astype(jnp.float32))
    grad_queries = grad_queries.reshape(row_count, D)
    grad_keys = grad_keys.reshape(row_count, D)
    grad_values = grad_values.reshape(row_count, D)
    grad_project = jnp.concatenate([grad_queries, grad_keys, grad_values], axis=1).astype(low)
    grad_input_w = jnp.dot(normed_low.T, grad_project, preferred_element_type=jnp.float32)
    grad_query_bias = lax.optimization_barrier(jnp.sum(grad_queries, axis=0))
    grad_value_bias = lax.optimization_barrier(jnp.sum(grad_values, axis=0))
    grad_normed = jnp.dot(grad_project, input_low.T, preferred_element_type=jnp.float32)
    back_a, grad_gain_a, grad_shift_a = norm_back(grad_normed, unit_a, scale_a, first_gain)
    grad_inputs = (grad_resid + back_a).astype(low).reshape(batch_size, S, D)
    flat_grad = jnp.concatenate([grad_gain_a, grad_shift_a, grad_input_w.reshape(-1), grad_query_bias, grad_value_bias, grad_output_w.reshape(-1), grad_output_bias, grad_gain_b, grad_shift_b, grad_up.reshape(-1), grad_up_bias, grad_down.reshape(-1), grad_down_bias])
    return (outputs, grad_inputs, flat_grad)

def adamw_update(weights, first_moment, second_moment, gradient):
    first_new = 0.9 * first_moment + 0.1 * gradient
    second_new = 0.99 * second_moment + 0.01 * gradient * gradient
    first_hat = first_new / (1.0 - 0.9 ** STEP)
    second_hat = second_new / (1.0 - 0.99 ** STEP)
    weights_new = weights - 0.02 * (first_hat / (jnp.sqrt(second_hat) + 1e-08) + 0.05 * weights)
    return (weights_new, first_new, second_new)

def reference(params, moment1, moment2, image_in, cotangent, image_counts):
    live_slots = (jnp.arange(SLOTS, dtype=jnp.int32)[None, :] < image_counts[:, None]).astype(jnp.float32)
    live_slots = live_slots.reshape(IMAGES)
    block_size = 8 * SLOTS
    turn_count = IMAGES // block_size

    def scan_step(grad_total, pieces):
        images, upstream, live_images = pieces
        live_rows = jnp.broadcast_to(live_images[:, None], (block_size, S)).reshape(block_size * S, 1)
        outputs, grad_inputs, flat_grad = block_pass(params, images, upstream, live_rows)
        return (grad_total + flat_grad, (outputs, grad_inputs))
    grad_total, (outputs, grad_inputs) = lax.scan(scan_step, jnp.zeros((PARAMS,), jnp.float32), (image_in.reshape(turn_count, block_size, S, D), cotangent.reshape(turn_count, block_size, S, D), live_slots.reshape(turn_count, block_size)))
    param_grad = grad_total * (1.0 / IMAGES)
    new_params, new_first, new_second = adamw_update(params, moment1, moment2, param_grad)
    return (outputs.reshape(IMAGES, S, D), grad_inputs.reshape(IMAGES, S, D), param_grad, new_params, new_first, new_second)
```

```python
import functools
import math

import jax
import jax.numpy as jnp
from jax import lax
from jax.experimental import pallas as pl
from jax.experimental.pallas import tpu as pltpu
from jax.sharding import PartitionSpec as P

D = 384
HEADS = 6
HEAD_DIM = 64
FF = 1536
STEP = 5
LANES = 128
MESH = pl.DeviceIdType.MESH
LOW = jnp.bfloat16
F32 = jnp.float32

SEGMENTS = [
    ("gain_a", 1, D),
    ("shift_a", 1, D),
    ("input", D, 3 * D),
    ("query_bias", 1, D),
    ("value_bias", 1, D),
    ("output", D, D),
    ("output_bias", 1, D),
    ("gain_b", 1, D),
    ("shift_b", 1, D),
    ("up", D, FF),
    ("up_bias", 1, FF),
    ("down", FF, D),
    ("down_bias", 1, D),
]


def starts_of():
    row, table = 0, {}
    for name, rows, columns in SEGMENTS:
        table[name] = row
        row += rows * columns // LANES
    return table


STARTS = starts_of()


class Layout:
    def __init__(self, shard, group, dp):
        self.real = shard // LANES
        self.group = group
        self.dp = dp
        unit = 8 * dp
        units = -(-self.real // unit)
        self.chunks = max(n for n in range(1, 12) if units % n == 0)
        self.padded = units * unit
        self.chunk = self.padded // self.chunks

    def pieces(self, start, stride, count):
        i, found = 0, []
        while i < count:
            row = start + stride * i
            shard = row // self.real
            n = min(count - i, ((shard + 1) * self.real - 1 - row) // stride + 1)
            found.append((shard * self.padded + row - shard * self.real, i, n))
            i += n
        return found


def gather_kernel(lay, own_ref, full_ref, sx, rx, sy, ry, sc, rc, so, ro, local_sem):
    d, g = lax.axis_index("dp"), lax.axis_index("group")
    half = d % 2
    core = {"dp": d, "group": g + 1 - 2 * (g % 2)}
    far_g = g + 2 - 4 * ((g // 2) % 2)
    far = {"dp": d, "group": far_g}
    side = {"dp": d + 1 - 2 * half, "group": g}
    barrier = pltpu.get_barrier_semaphore()
    for other in (core, far, side):
        pl.semaphore_signal(barrier, inc=1, device_id=other, device_id_type=MESH)
    pl.semaphore_wait(barrier, 3)

    piece = lay.chunk // 2
    half_rows = lay.padded // 2

    def rows(which, c):
        return pl.ds(pl.multiple_of(which * half_rows + c * piece, 8), piece)

    def send(src, shard, rows_at, s, r, other):
        copy = pltpu.make_async_remote_copy(
            src_ref=src,
            dst_ref=full_ref.at[shard, rows_at],
            send_sem=s,
            recv_sem=r,
            device_id=other,
            device_id_type=MESH,
        )
        copy.start()
        return copy

    def arrival(shard, rows_at, s, r, other):
        return pltpu.make_async_remote_copy(
            src_ref=full_ref.at[shard, rows_at],
            dst_ref=full_ref.at[shard, rows_at],
            send_sem=s,
            recv_sem=r,
            device_id=other,
            device_id_type=MESH,
        )

    sends = []
    xs = []
    for c in range(lay.chunks):
        at = rows(half, c)
        xs.append(send(own_ref.at[at], g, at, sx.at[c], rx.at[c], far))
    mine = pltpu.make_async_copy(own_ref, full_ref.at[g], local_sem)
    mine.start()
    own = pltpu.make_async_remote_copy(
        src_ref=own_ref,
        dst_ref=full_ref.at[g],
        send_sem=so,
        recv_sem=ro,
        device_id=core,
        device_id_type=MESH,
    )
    own.start()
    ys, cs = [], []
    for c in range(lay.chunks):
        at = rows(half, c)
        arrival(far_g, at, sx.at[c], rx.at[c], far).wait_recv()
        ys.append(send(full_ref.at[far_g, at], far_g, at, sy.at[c], ry.at[c], side))
        cs.append(send(full_ref.at[far_g, at], far_g, at, sc.at[0, c], rc.at[0, c], core))
    for c in range(lay.chunks):
        at = rows(1 - half, c)
        arrival(far_g, at, sy.at[c], ry.at[c], side).wait_recv()
        cs.append(send(full_ref.at[far_g, at], far_g, at, sc.at[1, c], rc.at[1, c], core))
    for copy in xs + ys:
        copy.wait_send()
    for copy in cs:
        copy.wait()
    own.wait()
    mine.wait()


def gather(lay, own):
    n = lay.chunks
    dma = pltpu.SemaphoreType.DMA
    return pl.pallas_call(
        functools.partial(gather_kernel, lay),
        out_shape=jax.ShapeDtypeStruct((lay.group, lay.padded, LANES), F32),
        in_specs=[pl.BlockSpec(memory_space=pl.ANY)],
        out_specs=pl.BlockSpec(memory_space=pl.ANY),
        scratch_shapes=[
            dma((n,)), dma((n,)), dma((n,)), dma((n,)), dma((2, n)), dma((2, n)), dma, dma, dma,
        ],
        compiler_params=pltpu.CompilerParams(collective_id=0, has_side_effects=True),
        name="gather_params",
    )(own)


def reduce_kernel(lay, grad_ref, out_ref, near, total, shifted, far_in, half_in, s_sem, r_sem):
    d, g = lax.axis_index("dp"), lax.axis_index("group")
    x, core = g // 2, g % 2
    bits = []
    step = 1
    while step < lay.dp:
        bits.append((d // step) % 2)
        step *= 2
    core_dev = {"dp": d, "group": 2 * x + 1 - core}
    far_dev = {"dp": d, "group": 2 * (1 - x) + core}
    dp_dev = [{"dp": d + (1 - 2 * b) * 2**k, "group": g} for k, b in enumerate(bits)]
    barrier = pltpu.get_barrier_semaphore()
    partners = [core_dev, far_dev] + dp_dev
    for other in partners:
        pl.semaphore_signal(barrier, inc=1, device_id=other, device_id_type=MESH)
    pl.semaphore_wait(barrier, len(partners))

    levels = len(bits)
    size = lay.chunk
    keep = [0]
    for k in range(levels):
        keep.append(keep[k] + bits[k] * (size >> (k + 1)))
    recv_at = []
    base = 0
    for k in range(levels):
        recv_at.append(base)
        base += size >> (k + 1)

    started = {}

    def send(phase, c, src, dst, other):
        copy = pltpu.make_async_remote_copy(
            src_ref=src,
            dst_ref=dst,
            send_sem=s_sem.at[phase, c],
            recv_sem=r_sem.at[phase, c],
            device_id=other,
            device_id_type=MESH,
        )
        copy.start()
        started[phase, c] = copy

    def at(offset, count):
        return pl.ds(pl.multiple_of(offset, 8), count)

    def stage(phase, c):
        begin = c * size
        whole = pl.ds(begin, size)
        if phase > 0:
            started[phase - 1, c].wait_recv()
        if phase == 0:
            send(0, c, grad_ref.at[:, 1 - core, whole], near.at[:, whole], core_dev)
        elif phase == 1:
            shifted[whole] = grad_ref[1 - x, core, whole] + near[1 - x, whole]
            send(1, c, shifted.at[whole], far_in.at[whole], far_dev)
        elif phase < 2 + levels:
            k = phase - 2
            part = size >> k
            if k == 0:
                total[whole] = grad_ref[x, core, whole] + near[x, whole] + far_in[whole]
            else:
                here = at(begin + keep[k], part)
                total[here] = total[here] + half_in[c, recv_at[k - 1] : recv_at[k - 1] + part]
            half = part // 2
            other = keep[k] + (1 - bits[k]) * half
            send(
                phase,
                c,
                total.at[at(begin + other, half)],
                half_in.at[c, recv_at[k] : recv_at[k] + half],
                dp_dev[k],
            )
        else:
            k = levels - 1 - (phase - 2 - levels)
            if k == levels - 1:
                part = size >> levels
                here = at(begin + keep[levels], part)
                out_ref[here] = total[here] + half_in[c, recv_at[k] : recv_at[k] + part]
            if k >= 0:
                here = at(begin + keep[k + 1], size >> (k + 1))
                send(phase, c, out_ref.at[here], out_ref.at[here], dp_dev[k])

    last = 2 + 2 * levels
    for turn in range(lay.chunks + last):
        for phase in range(last, -1, -1):
            c = turn - phase
            if 0 <= c < lay.chunks:
                stage(phase, c)
    for copy in started.values():
        copy.wait_send()


def reduce(lay, grads):
    levels = lay.dp.bit_length() - 1
    phases = 2 + 2 * levels
    dma = pltpu.SemaphoreType.DMA
    parts = sum(lay.chunk >> (k + 1) for k in range(levels))
    vmem = pl.BlockSpec(memory_space=pltpu.VMEM)
    return pl.pallas_call(
        functools.partial(reduce_kernel, lay),
        out_shape=jax.ShapeDtypeStruct((lay.padded, LANES), F32),
        in_specs=[vmem],
        out_specs=vmem,
        scratch_shapes=[
            pltpu.VMEM((2, lay.padded, LANES), F32),
            pltpu.VMEM((lay.padded, LANES), F32),
            pltpu.VMEM((lay.padded, LANES), F32),
            pltpu.VMEM((lay.padded, LANES), F32),
            pltpu.VMEM((lay.chunks, parts, LANES), F32),
            dma((phases, lay.chunks)),
            dma((phases, lay.chunks)),
        ],
        compiler_params=pltpu.CompilerParams(
            collective_id=1, has_side_effects=True, vmem_limit_bytes=40 * 2**20
        ),
        name="reduce_grads",
    )(grads.reshape(2, 2, lay.padded, LANES))


def dot(a, b):
    return jnp.dot(a, b, preferred_element_type=F32)


def dot_nt(a, b):
    return lax.dot_general(a, b, (((1,), (1,)), ((), ())), preferred_element_type=F32)


def dot_tn(a, b):
    return lax.dot_general(a, b, (((0,), (0,)), ((), ())), preferred_element_type=F32)


def column_sum(v):
    return jnp.sum(v, axis=0, keepdims=True)


def norm(values):
    middle = jnp.mean(values, axis=-1, keepdims=True)
    off = values - middle
    spread = jnp.mean(off * off, axis=-1, keepdims=True)
    scaled = lax.rsqrt(spread + 1e-06)
    return off * scaled, scaled


def norm_back(upstream, unit, scaled, gain):
    inner = upstream * gain
    return scaled * (
        inner
        - jnp.mean(inner, axis=-1, keepdims=True)
        - unit * jnp.mean(inner * unit, axis=-1, keepdims=True)
    )


def block_kernel(
    lay, counts_ref, full_ref, image_ref, cot_ref, out_ref, gin_ref, grad_ref,
    w_in, w_out, w_up, w_down, stage, x_s, g_s, unit_a, low_a, q_s, k_s, v_s, probs_s,
    mixed_s, resid_s, gm_s, gp_s, gacc_s,
):
    slots, tokens, _ = image_ref.shape
    pad = x_s.shape[0] // slots

    def weight(name, dst):
        start = STARTS[name]
        rows, columns = dst.shape
        stride = columns // LANES
        for j in range(stride):
            found = lay.pieces(start + j, stride, rows)
            lanes = slice(j * LANES, (j + 1) * LANES)
            if len(found) == 1:
                at = found[0][0]
                dst[:, lanes] = full_ref[pl.ds(at, rows, stride=stride), :].astype(LOW)
            else:
                for at, i, n in found:
                    stage[i : i + n, :] = full_ref[pl.ds(at, n, stride=stride), :]
                dst[:, lanes] = stage[0:rows, :].astype(LOW)

    def vector(name, skip=0, columns=D):
        start = STARTS[name] + skip // LANES
        found = []
        for j in range(columns // LANES):
            at = lay.pieces(start + j, 1, 1)[0][0]
            found.append(full_ref[at : at + 1, :])
        return jnp.concatenate(found, axis=1)

    def put_vector(name, value, skip=0):
        start = STARTS[name] + skip // LANES
        for j in range(value.shape[1] // LANES):
            at = lay.pieces(start + j, 1, 1)[0][0]
            grad_ref[at : at + 1, :] = value[:, j * LANES : (j + 1) * LANES]

    def put_weight(name, stride, value, first_row=0, first_column=0):
        rows, columns = value.shape
        start = STARTS[name] + first_row * stride + first_column // LANES
        for j in range(columns // LANES):
            found = lay.pieces(start + j, stride, rows)
            part = value[:, j * LANES : (j + 1) * LANES]
            if len(found) == 1:
                grad_ref[pl.ds(found[0][0], rows, stride=stride), :] = part
            else:
                stage[0:rows, :] = part
                for at, i, n in found:
                    grad_ref[pl.ds(at, n, stride=stride), :] = stage[i : i + n, :]

    weight("input", w_in)
    weight("output", w_out)
    weight("up", w_up)
    weight("down", w_down)
    for s in range(lay.group):
        tail = s * lay.padded + lay.real
        grad_ref[tail : (s + 1) * lay.padded, :] = jnp.zeros((lay.padded - lay.real, LANES), F32)

    count = counts_ref[0]
    x_s[...] = jnp.zeros_like(x_s)
    g_s[...] = jnp.zeros_like(g_s)
    lives = []
    for b in range(slots):
        live = jnp.where(b < count, 1.0, 0.0).astype(F32)
        lives.append(live)
        x_s[b * pad : b * pad + tokens, :] = image_ref[b].astype(F32)
        g_s[b * pad : b * pad + tokens, :] = cot_ref[b].astype(F32) * live

    unit, scale_a = norm(x_s[...])
    unit_a[...] = unit
    low_a[...] = (unit * vector("gain_a") + vector("shift_a")).astype(LOW)
    q_s[...] = (dot(low_a[...], w_in[:, 0:D]) + vector("query_bias")).astype(LOW)
    k_s[...] = dot(low_a[...], w_in[:, D : 2 * D]).astype(LOW)
    v_s[...] = (dot(low_a[...], w_in[:, 2 * D :]) + vector("value_bias")).astype(LOW)

    factor = HEAD_DIM ** (-0.5)
    first = lax.broadcasted_iota(jnp.int32, (pad, LANES), 1) < HEAD_DIM
    valid = lax.broadcasted_iota(jnp.int32, (pad, pad), 1) < tokens
    zero = jnp.zeros((pad, LANES), LOW)

    def only(value, h):
        return jnp.where(first, value, zero) if h == 0 else jnp.where(first, zero, value)

    pairs = HEADS // 2
    for b in range(slots):
        rows = slice(b * pad, (b + 1) * pad)
        for p in range(pairs):
            lanes = slice(p * LANES, (p + 1) * LANES)
            q, k, v = q_s[rows, lanes], k_s[rows, lanes], v_s[rows, lanes]
            parts = []
            for h in range(2):
                scores = dot_nt(only(q, h), k) * factor
                scores = jnp.where(valid, scores, -jnp.inf)
                top = jnp.max(scores, axis=-1, keepdims=True)
                e = jnp.exp(scores - top)
                probs = e * (1.0 / jnp.sum(e, axis=-1, keepdims=True))
                probs_s[(b * pairs + p) * 2 + h] = probs
                parts.append(dot(probs.astype(LOW), v))
            mixed_s[rows, lanes] = jnp.where(first, parts[0], parts[1]).astype(LOW)

    residual = x_s[...] + dot(mixed_s[...], w_out[...]) + vector("output_bias")
    resid_s[...] = residual
    unit_b, scale_b = norm(residual)
    hidden = (unit_b * vector("gain_b") + vector("shift_b")).astype(LOW)
    grad_low = g_s[...].astype(LOW)
    final = resid_s[...] + vector("down_bias")
    for j in range(FF // D):
        at = slice(j * D, (j + 1) * D)
        pre = dot(hidden, w_up[:, at]) + vector("up_bias", j * D)
        cdf = 0.5 * (1.0 + lax.erf(pre * (1.0 / math.sqrt(2.0))))
        act = (pre * cdf).astype(LOW)
        density = jnp.exp(-0.5 * pre * pre) * (1.0 / math.sqrt(2.0 * math.pi))
        final = final + dot(act, w_down[at, :])
        grad_pre = dot_nt(grad_low, w_down[at, :]) * (cdf + pre * density)
        put_vector("up_bias", column_sum(grad_pre), j * D)
        grad_pre_low = grad_pre.astype(LOW)
        put_weight("down", D // LANES, dot_tn(act, grad_low), first_row=j * D)
        put_weight("up", FF // LANES, dot_tn(hidden, grad_pre_low), first_column=j * D)
        back = dot_nt(grad_pre_low, w_up[:, at])
        if j == 0:
            gacc_s[...] = back
        else:
            gacc_s[...] += back
    for b in range(slots):
        out_ref[b] = (final[b * pad : b * pad + tokens, :] * lives[b]).astype(LOW)
    put_vector("down_bias", column_sum(g_s[...]))

    grad_hidden = gacc_s[...]
    put_vector("gain_b", column_sum(grad_hidden * unit_b))
    put_vector("shift_b", column_sum(grad_hidden))
    grad_resid = g_s[...] + norm_back(grad_hidden, unit_b, scale_b, vector("gain_b"))
    resid_s[...] = grad_resid
    put_vector("output_bias", column_sum(grad_resid))
    resid_low = grad_resid.astype(LOW)
    put_weight("output", D // LANES, dot_tn(mixed_s[...], resid_low))
    gm_s[...] = dot_nt(resid_low, w_out[...]).astype(LOW)

    query_sum = [0.0] * pairs
    value_sum = [0.0] * pairs
    for b in range(slots):
        rows = slice(b * pad, (b + 1) * pad)
        for p in range(pairs):
            lanes = slice(p * LANES, (p + 1) * LANES)
            q, k, v, gm = q_s[rows, lanes], k_s[rows, lanes], v_s[rows, lanes], gm_s[rows, lanes]
            gq, gk, gv = [], [], []
            for h in range(2):
                probs = probs_s[(b * pairs + p) * 2 + h]
                grad_probs = dot_nt(only(gm, h), v)
                gv.append(dot_tn(probs.astype(LOW), gm))
                centre = jnp.sum(grad_probs * probs, axis=-1, keepdims=True)
                grad_scores = (probs * (grad_probs - centre) * factor).astype(LOW)
                gq.append(dot(grad_scores, k))
                gk.append(dot_tn(grad_scores, q))
            both = [jnp.where(first, pair[0], pair[1]) for pair in (gq, gk, gv)]
            query_sum[p] = query_sum[p] + column_sum(both[0])
            value_sum[p] = value_sum[p] + column_sum(both[2])
            for c in range(3):
                gp_s[rows, c * D + p * LANES : c * D + (p + 1) * LANES] = both[c].astype(LOW)
    put_vector("query_bias", jnp.concatenate(query_sum, axis=1))
    put_vector("value_bias", jnp.concatenate(value_sum, axis=1))
    for c in range(3):
        at = slice(c * D, (c + 1) * D)
        put_weight(
            "input", 3 * D // LANES, dot_tn(low_a[...], gp_s[:, at]), first_column=c * D
        )
    grad_normed = dot_nt(gp_s[...], w_in[...])
    put_vector("gain_a", column_sum(grad_normed * unit_a[...]))
    put_vector("shift_a", column_sum(grad_normed))
    grad_in = resid_s[...] + norm_back(grad_normed, unit_a[...], scale_a, vector("gain_a"))
    for b in range(slots):
        gin_ref[b] = grad_in[b * pad : b * pad + tokens, :].astype(LOW)


def block_pass(lay, full, images, upstream, counts):
    slots, tokens, _ = images.shape
    pad = -(-tokens // 16) * 16
    rows = slots * pad
    vmem = pl.BlockSpec(memory_space=pltpu.VMEM)
    flat = (lay.group * lay.padded, LANES)
    low = lambda *shape: pltpu.VMEM(shape, LOW)
    wide = lambda *shape: pltpu.VMEM(shape, F32)
    return pl.pallas_call(
        functools.partial(block_kernel, lay),
        out_shape=(
            jax.ShapeDtypeStruct(images.shape, LOW),
            jax.ShapeDtypeStruct(images.shape, LOW),
            jax.ShapeDtypeStruct(flat, F32),
        ),
        in_specs=[pl.BlockSpec(memory_space=pltpu.SMEM), vmem, vmem, vmem],
        out_specs=(vmem, vmem, vmem),
        scratch_shapes=[
            low(D, 3 * D), low(D, D), low(D, FF), low(FF, D), wide(FF, LANES),
            wide(rows, D), wide(rows, D), wide(rows, D), low(rows, D),
            low(rows, D), low(rows, D), low(rows, D),
            wide(slots * HEADS, pad, pad),
            low(rows, D), wide(rows, D), low(rows, D), low(rows, 3 * D), wide(rows, D),
        ],
        compiler_params=pltpu.CompilerParams(vmem_limit_bytes=56 * 2**20),
        name="block_pass",
    )(counts, full.reshape(flat), images, upstream)


def adamw_update(weights, first_moment, second_moment, gradient):
    first_new = 0.9 * first_moment + 0.1 * gradient
    second_new = 0.99 * second_moment + 0.01 * gradient * gradient
    first_hat = first_new / (1.0 - 0.9**STEP)
    second_hat = second_new / (1.0 - 0.99**STEP)
    weights_new = weights - 0.02 * (first_hat / (jnp.sqrt(second_hat) + 1e-08) + 0.05 * weights)
    return (weights_new, first_new, second_new)


def on_device(params, moment1, moment2, image_in, cotangent, image_counts):
    group, dp = lax.axis_size("group"), lax.axis_size("dp")
    lay = Layout(params.shape[0], group, dp)
    own = jnp.pad(params, (0, (lay.padded - lay.real) * LANES)).reshape(lay.padded, LANES)
    full = gather(lay, own)
    outputs, grad_inputs, grads = block_pass(lay, full, image_in, cotangent, image_counts)
    summed = reduce(lay, grads)
    images = image_in.shape[0] * group * dp
    grad_shard = summed.reshape(-1)[: params.shape[0]] * (1.0 / images)
    new_params, new_first, new_second = adamw_update(params, moment1, moment2, grad_shard)
    return (outputs, grad_inputs, grad_shard, new_params, new_first, new_second)


def solution(mesh):
    placed = (
        P("group"),
        P("group"),
        P("group"),
        P(("dp", "group"), None, None),
        P(("dp", "group"), None, None),
        P(("dp", "group")),
    )
    return jax.shard_map(
        on_device,
        mesh=mesh,
        in_specs=placed,
        out_specs=(
            P(("dp", "group"), None, None),
            P(("dp", "group"), None, None),
            P("group"),
            P("group"),
            P("group"),
            P("group"),
        ),
        check_vma=False,
    )
```

```python
import functools
import math

import jax
import jax.numpy as jnp
from jax import lax
from jax.experimental import pallas as pl
from jax.experimental.pallas import tpu as pltpu
from jax.sharding import PartitionSpec as P

D = 384
HEADS = 6
HEAD_DIM = 64
FF = 1536
STEP = 5
LANES = 128
MOST_CHUNKS = 14
MOST_PARTS = 8
IN_FLIGHT = 2
FAR_AHEAD = 2
SIDE_AHEAD = 2
WIDE_AHEAD = 2
MESH = pl.DeviceIdType.MESH
LOW = jnp.bfloat16
F32 = jnp.float32

SEGMENTS = [
    ("gain_a", 1, D),
    ("shift_a", 1, D),
    ("input", D, 3 * D),
    ("query_bias", 1, D),
    ("value_bias", 1, D),
    ("output", D, D),
    ("output_bias", 1, D),
    ("gain_b", 1, D),
    ("shift_b", 1, D),
    ("up", D, FF),
    ("up_bias", 1, FF),
    ("down", FF, D),
    ("down_bias", 1, D),
]


def starts_of():
    row, table = 0, {}
    for name, rows, columns in SEGMENTS:
        table[name] = row
        row += rows * columns // LANES
    return table


STARTS = starts_of()


class Layout:
    def __init__(self, shard, group, dp):
        self.real = shard // LANES
        self.group = group
        self.dp = dp
        unit = 8 * dp
        least = -(-self.real // unit)
        self.chunks, units = max(
            (n, -units)
            for units in range(least, least + least // 16 + 1)
            for n in range(1, MOST_CHUNKS + 1)
            if units % n == 0
        )
        self.padded = -units * unit
        self.chunk = self.padded // self.chunks
        half = self.padded // 16
        self.parts = max(n for n in range(1, MOST_PARTS + 1) if half % n == 0)

    def pieces(self, start, stride, count):
        i, found = 0, []
        while i < count:
            row = start + stride * i
            shard = row // self.real
            n = min(count - i, ((shard + 1) * self.real - 1 - row) // stride + 1)
            found.append((shard * self.padded + row - shard * self.real, i, n))
            i += n
        return found


def gather_kernel(lay, own_ref, full_ref, sx, rx, sy, ry, sc, rc, so, ro, local_sem):
    d, g = lax.axis_index("dp"), lax.axis_index("group")
    half = d % 2
    core = {"dp": d, "group": g + 1 - 2 * (g % 2)}
    far_g = g + 2 - 4 * ((g // 2) % 2)
    far = {"dp": d, "group": far_g}
    side = {"dp": d + 1 - 2 * half, "group": g}
    barrier = pltpu.get_barrier_semaphore()
    for other in (core, far, side):
        pl.semaphore_signal(barrier, inc=1, device_id=other, device_id_type=MESH)
    pl.semaphore_wait(barrier, 3)

    piece = lay.padded // 2 // lay.parts
    half_rows = lay.padded // 2

    def rows(which, c):
        return pl.ds(pl.multiple_of(which * half_rows + c * piece, 8), piece)

    def send(src, shard, rows_at, s, r, other):
        copy = pltpu.make_async_remote_copy(
            src_ref=src,
            dst_ref=full_ref.at[shard, rows_at],
            send_sem=s,
            recv_sem=r,
            device_id=other,
            device_id_type=MESH,
        )
        copy.start()
        return copy

    def arrival(shard, rows_at, s, r, other):
        return pltpu.make_async_remote_copy(
            src_ref=full_ref.at[shard, rows_at],
            dst_ref=full_ref.at[shard, rows_at],
            send_sem=s,
            recv_sem=r,
            device_id=other,
            device_id_type=MESH,
        )

    xs, ys, cs = [], [], []

    def send_far(c):
        at = rows(half, c)
        xs.append(send(own_ref.at[at], g, at, sx.at[c], rx.at[c], far))

    def pass_far(c):
        at = rows(half, c)
        arrival(far_g, at, sx.at[c], rx.at[c], far).wait_recv()
        ys.append(send(full_ref.at[far_g, at], far_g, at, sy.at[c], ry.at[c], side))
        cs.append(send(full_ref.at[far_g, at], far_g, at, sc.at[0, c], rc.at[0, c], core))

    def pass_side(c):
        at = rows(1 - half, c)
        arrival(far_g, at, sy.at[c], ry.at[c], side).wait_recv()
        cs.append(send(full_ref.at[far_g, at], far_g, at, sc.at[1, c], rc.at[1, c], core))

    for c in range(min(IN_FLIGHT, lay.parts)):
        send_far(c)
    mine = pltpu.make_async_copy(own_ref, full_ref.at[g], local_sem)
    mine.start()
    own = pltpu.make_async_remote_copy(
        src_ref=own_ref,
        dst_ref=full_ref.at[g],
        send_sem=so,
        recv_sem=ro,
        device_id=core,
        device_id_type=MESH,
    )
    own.start()
    for c in range(lay.parts):
        pass_far(c)
        if c + IN_FLIGHT < lay.parts:
            send_far(c + IN_FLIGHT)
        if c >= IN_FLIGHT:
            pass_side(c - IN_FLIGHT)
    for c in range(max(lay.parts - IN_FLIGHT, 0), lay.parts):
        pass_side(c)
    for copy in xs + ys:
        copy.wait_send()
    for copy in cs:
        copy.wait()
    own.wait()
    mine.wait()


def gather(lay, own):
    n = lay.parts
    dma = pltpu.SemaphoreType.DMA
    return pl.pallas_call(
        functools.partial(gather_kernel, lay),
        out_shape=jax.ShapeDtypeStruct((lay.group, lay.padded, LANES), F32),
        in_specs=[pl.BlockSpec(memory_space=pltpu.VMEM)],
        out_specs=pl.BlockSpec(memory_space=pl.ANY),
        scratch_shapes=[
            dma((n,)), dma((n,)), dma((n,)), dma((n,)), dma((2, n)), dma((2, n)), dma, dma, dma,
        ],
        compiler_params=pltpu.CompilerParams(collective_id=0, has_side_effects=True),
        name="gather_params",
    )(own)


def radices_of(dp):
    found, rest = [], dp
    if rest % 2 == 0:
        found.append(2)
        rest //= 2
    while rest > 1:
        r = next(n for n in (4, 2, rest) if rest % n == 0)
        found.append(r)
        rest //= r
    return found


def reduce_kernel(lay, grad_ref, out_ref, near, total, shifted, far_in, part_in, s_sem, r_sem):
    d, g = lax.axis_index("dp"), lax.axis_index("group")
    x, core = g // 2, g % 2
    core_dev = {"dp": d, "group": 2 * x + 1 - core}
    far_dev = {"dp": d, "group": 2 * (1 - x) + core}
    levels, step = [], 1
    for radix in radices_of(lay.dp):
        digit = (d // step) % radix
        others = []
        for o in range(1, radix):
            digit_o = (digit + o) % radix
            others.append((digit_o, {"dp": d + (digit_o - digit) * step, "group": g}))
        levels.append((radix, digit, others))
        step *= radix
    barrier = pltpu.get_barrier_semaphore()
    partners = [core_dev, far_dev] + [dev for _, _, others in levels for _, dev in others]
    for other in partners:
        pl.semaphore_signal(barrier, inc=1, device_id=other, device_id_type=MESH)
    pl.semaphore_wait(barrier, len(partners))

    depth = len(levels)
    held, keep, slot, base = [lay.chunk], [0], [], 0
    for radix, digit, others in levels:
        part = held[-1] // radix
        keep.append(keep[-1] + digit * part)
        held.append(part)
        slot.append(base)
        base += part * (radix - 1)
    started = {}
    sems = {}

    def send(phase, o, c, src, dst, other):
        at = sems.setdefault((phase, o), len(sems))
        copy = pltpu.make_async_remote_copy(
            src_ref=src,
            dst_ref=dst,
            send_sem=s_sem.at[at, c],
            recv_sem=r_sem.at[at, c],
            device_id=other,
            device_id_type=MESH,
        )
        copy.start()
        started.setdefault((phase, c), []).append(copy)

    def at(offset, count):
        return pl.ds(pl.multiple_of(offset, 8), count)

    def arrived(k, c):
        radix, part = levels[k][0], held[k + 1]
        found = [part_in[c, slot[k] + o * part : slot[k] + (o + 1) * part] for o in range(radix - 1)]
        return functools.reduce(lambda a, b: a + b, found)

    def stage(phase, c):
        begin = c * lay.chunk
        whole = pl.ds(begin, lay.chunk)
        for copy in started.get((phase - 1, c), []):
            copy.wait_recv()
        if phase == 0:
            send(0, 0, c, grad_ref.at[:, 1 - core, whole], near.at[:, whole], core_dev)
        elif phase == 1:
            shifted[whole] = grad_ref[1 - x, core, whole] + near[1 - x, whole]
            send(1, 0, c, shifted.at[whole], far_in.at[whole], far_dev)
        elif phase < 2 + depth:
            k = phase - 2
            if k == 0:
                total[whole] = grad_ref[x, core, whole] + near[x, whole] + far_in[whole]
            else:
                here = at(begin + keep[k], held[k])
                total[here] = total[here] + arrived(k - 1, c)
            part = held[k + 1]
            for o, (digit, dev) in enumerate(levels[k][2]):
                send(
                    phase,
                    o,
                    c,
                    total.at[at(begin + keep[k] + digit * part, part)],
                    part_in.at[c, slot[k] + o * part : slot[k] + (o + 1) * part],
                    dev,
                )
        else:
            k = depth - 1 - (phase - 2 - depth)
            if k == depth - 1:
                here = at(begin + keep[depth], held[depth])
                out_ref[here] = total[here] + arrived(k, c)
            if k >= 0:
                here = at(begin + keep[k + 1], held[k + 1])
                for o, (_, dev) in enumerate(levels[k][2]):
                    send(phase, o, c, out_ref.at[here], out_ref.at[here], dev)

    last = 2 + 2 * depth
    late = [0, 1, 1 + FAR_AHEAD, 1 + FAR_AHEAD + SIDE_AHEAD]
    while len(late) < last:
        late.append(late[-1] + WIDE_AHEAD)
    late.append(late[-1] + SIDE_AHEAD)
    order = [1, 0] + list(range(last, 1, -1))
    for turn in range(lay.chunks + late[last]):
        for phase in order:
            c = turn - late[phase]
            if 0 <= c < lay.chunks:
                stage(phase, c)
    for copies in started.values():
        for copy in copies:
            copy.wait_send()


def reduce(lay, grads):
    radices = radices_of(lay.dp)
    copies = 2 + 2 * sum(r - 1 for r in radices)
    parts, held = 0, lay.chunk
    for r in radices:
        held //= r
        parts += held * (r - 1)
    dma = pltpu.SemaphoreType.DMA
    vmem = pl.BlockSpec(memory_space=pltpu.VMEM)
    return pl.pallas_call(
        functools.partial(reduce_kernel, lay),
        out_shape=jax.ShapeDtypeStruct((lay.padded, LANES), F32),
        in_specs=[vmem],
        out_specs=vmem,
        scratch_shapes=[
            pltpu.VMEM((2, lay.padded, LANES), F32),
            pltpu.VMEM((lay.padded, LANES), F32),
            pltpu.VMEM((lay.padded, LANES), F32),
            pltpu.VMEM((lay.padded, LANES), F32),
            pltpu.VMEM((lay.chunks, parts, LANES), F32),
            dma((copies, lay.chunks)),
            dma((copies, lay.chunks)),
        ],
        compiler_params=pltpu.CompilerParams(
            collective_id=1, has_side_effects=True, vmem_limit_bytes=28 * 2**20
        ),
        name="reduce_grads",
    )(grads.reshape(2, 2, lay.padded, LANES))


def dot(a, b):
    return jnp.dot(a, b, preferred_element_type=F32)


def dot_nt(a, b):
    return lax.dot_general(a, b, (((1,), (1,)), ((), ())), preferred_element_type=F32)


def dot_tn(a, b):
    return lax.dot_general(a, b, (((0,), (0,)), ((), ())), preferred_element_type=F32)


def column_sum(v):
    return jnp.sum(v, axis=0, keepdims=True)


def norm(values):
    middle = jnp.mean(values, axis=-1, keepdims=True)
    off = values - middle
    spread = jnp.mean(off * off, axis=-1, keepdims=True)
    scaled = lax.rsqrt(spread + 1e-06)
    return off * scaled, scaled


def norm_back(upstream, unit, scaled, gain):
    inner = upstream * gain
    return scaled * (
        inner
        - jnp.mean(inner, axis=-1, keepdims=True)
        - unit * jnp.mean(inner * unit, axis=-1, keepdims=True)
    )


def block_kernel(
    lay, counts_ref, full_ref, image_ref, cot_ref, out_ref, gin_ref, grad_ref,
    w_in, w_out, w_up, w_down, stage, x_s, g_s, unit_a, low_a, q_s, k_s, v_s, probs_s,
    mixed_s, resid_s, gm_s, gp_s, gacc_s,
):
    tokens, slots, _ = image_ref.shape
    pad = x_s.shape[0] // slots

    def weight(name, dst):
        start = STARTS[name]
        rows, columns = dst.shape
        stride = columns // LANES
        for j in range(stride):
            found = lay.pieces(start + j, stride, rows)
            lanes = slice(j * LANES, (j + 1) * LANES)
            if len(found) == 1:
                at = found[0][0]
                dst[:, lanes] = full_ref[pl.ds(at, rows, stride=stride), :].astype(LOW)
            else:
                for at, i, n in found:
                    stage[i : i + n, :] = full_ref[pl.ds(at, n, stride=stride), :]
                dst[:, lanes] = stage[0:rows, :].astype(LOW)

    def vector(name, skip=0, columns=D):
        start = STARTS[name] + skip // LANES
        found = []
        for j in range(columns // LANES):
            at = lay.pieces(start + j, 1, 1)[0][0]
            found.append(full_ref[at : at + 1, :])
        return jnp.concatenate(found, axis=1)

    def put_vector(name, value, skip=0):
        start = STARTS[name] + skip // LANES
        for j in range(value.shape[1] // LANES):
            at = lay.pieces(start + j, 1, 1)[0][0]
            grad_ref[at : at + 1, :] = value[:, j * LANES : (j + 1) * LANES]

    def put_weight(name, stride, value, first_row=0, first_column=0):
        rows, columns = value.shape
        start = STARTS[name] + first_row * stride + first_column // LANES
        for j in range(columns // LANES):
            found = lay.pieces(start + j, stride, rows)
            part = value[:, j * LANES : (j + 1) * LANES]
            if len(found) == 1:
                grad_ref[pl.ds(found[0][0], rows, stride=stride), :] = part
            else:
                stage[0:rows, :] = part
                for at, i, n in found:
                    grad_ref[pl.ds(at, n, stride=stride), :] = stage[i : i + n, :]

    weight("input", w_in)
    weight("output", w_out)
    weight("up", w_up)
    weight("down", w_down)
    for s in range(lay.group):
        tail = s * lay.padded + lay.real
        grad_ref[tail : (s + 1) * lay.padded, :] = jnp.zeros((lay.padded - lay.real, LANES), F32)

    count = counts_ref[0]
    x_s[...] = jnp.zeros_like(x_s)
    g_s[...] = jnp.zeros_like(g_s)
    lives = []
    for b in range(slots):
        live = jnp.where(b < count, 1.0, 0.0).astype(F32)
        lives.append(live)
        x_s[b * pad : b * pad + tokens, :] = image_ref[:, b, :].astype(F32)
        g_s[b * pad : b * pad + tokens, :] = cot_ref[:, b, :].astype(F32) * live

    unit, scale_a = norm(x_s[...])
    unit_a[...] = unit
    low_a[...] = (unit * vector("gain_a") + vector("shift_a")).astype(LOW)
    q_s[...] = (dot(low_a[...], w_in[:, 0:D]) + vector("query_bias")).astype(LOW)
    k_s[...] = dot(low_a[...], w_in[:, D : 2 * D]).astype(LOW)
    v_s[...] = (dot(low_a[...], w_in[:, 2 * D :]) + vector("value_bias")).astype(LOW)

    factor = HEAD_DIM ** (-0.5)
    first = lax.broadcasted_iota(jnp.int32, (pad, LANES), 1) < HEAD_DIM
    valid = lax.broadcasted_iota(jnp.int32, (pad, pad), 1) < tokens
    zero = jnp.zeros((pad, LANES), LOW)

    def only(value, h):
        return jnp.where(first, value, zero) if h == 0 else jnp.where(first, zero, value)

    pairs = HEADS // 2
    for b in range(slots):
        rows = slice(b * pad, (b + 1) * pad)
        for p in range(pairs):
            lanes = slice(p * LANES, (p + 1) * LANES)
            q, k, v = q_s[rows, lanes], k_s[rows, lanes], v_s[rows, lanes]
            parts = []
            for h in range(2):
                scores = dot_nt(only(q, h), k) * factor
                scores = jnp.where(valid, scores, -jnp.inf)
                top = jnp.max(scores, axis=-1, keepdims=True)
                e = jnp.exp(scores - top)
                probs = e * (1.0 / jnp.sum(e, axis=-1, keepdims=True))
                probs_s[(b * pairs + p) * 2 + h] = probs
                parts.append(dot(probs.astype(LOW), v))
            mixed_s[rows, lanes] = jnp.where(first, parts[0], parts[1]).astype(LOW)

    residual = x_s[...] + dot(mixed_s[...], w_out[...]) + vector("output_bias")
    resid_s[...] = residual
    unit_b, scale_b = norm(residual)
    hidden = (unit_b * vector("gain_b") + vector("shift_b")).astype(LOW)
    grad_low = g_s[...].astype(LOW)
    final = resid_s[...] + vector("down_bias")
    for j in range(FF // D):
        at = slice(j * D, (j + 1) * D)
        pre = dot(hidden, w_up[:, at]) + vector("up_bias", j * D)
        cdf = 0.5 * (1.0 + lax.erf(pre * (1.0 / math.sqrt(2.0))))
        act = (pre * cdf).astype(LOW)
        density = jnp.exp(-0.5 * pre * pre) * (1.0 / math.sqrt(2.0 * math.pi))
        final = final + dot(act, w_down[at, :])
        grad_pre = dot_nt(grad_low, w_down[at, :]) * (cdf + pre * density)
        put_vector("up_bias", column_sum(grad_pre), j * D)
        grad_pre_low = grad_pre.astype(LOW)
        put_weight("down", D // LANES, dot_tn(act, grad_low), first_row=j * D)
        put_weight("up", FF // LANES, dot_tn(hidden, grad_pre_low), first_column=j * D)
        back = dot_nt(grad_pre_low, w_up[:, at])
        if j == 0:
            gacc_s[...] = back
        else:
            gacc_s[...] += back
    for b in range(slots):
        out_ref[:, b, :] = (final[b * pad : b * pad + tokens, :] * lives[b]).astype(LOW)
    put_vector("down_bias", column_sum(g_s[...]))

    grad_hidden = gacc_s[...]
    put_vector("gain_b", column_sum(grad_hidden * unit_b))
    put_vector("shift_b", column_sum(grad_hidden))
    grad_resid = g_s[...] + norm_back(grad_hidden, unit_b, scale_b, vector("gain_b"))
    resid_s[...] = grad_resid
    put_vector("output_bias", column_sum(grad_resid))
    resid_low = grad_resid.astype(LOW)
    put_weight("output", D // LANES, dot_tn(mixed_s[...], resid_low))
    gm_s[...] = dot_nt(resid_low, w_out[...]).astype(LOW)

    query_sum = [0.0] * pairs
    value_sum = [0.0] * pairs
    for b in range(slots):
        rows = slice(b * pad, (b + 1) * pad)
        for p in range(pairs):
            lanes = slice(p * LANES, (p + 1) * LANES)
            q, k, v, gm = q_s[rows, lanes], k_s[rows, lanes], v_s[rows, lanes], gm_s[rows, lanes]
            gq, gk, gv = [], [], []
            for h in range(2):
                probs = probs_s[(b * pairs + p) * 2 + h]
                grad_probs = dot_nt(only(gm, h), v)
                gv.append(dot_tn(probs.astype(LOW), gm))
                centre = jnp.sum(grad_probs * probs, axis=-1, keepdims=True)
                grad_scores = (probs * (grad_probs - centre) * factor).astype(LOW)
                gq.append(dot(grad_scores, k))
                gk.append(dot_tn(grad_scores, q))
            both = [jnp.where(first, pair[0], pair[1]) for pair in (gq, gk, gv)]
            query_sum[p] = query_sum[p] + column_sum(both[0])
            value_sum[p] = value_sum[p] + column_sum(both[2])
            for c in range(3):
                gp_s[rows, c * D + p * LANES : c * D + (p + 1) * LANES] = both[c].astype(LOW)
    put_vector("query_bias", jnp.concatenate(query_sum, axis=1))
    put_vector("value_bias", jnp.concatenate(value_sum, axis=1))
    for c in range(3):
        at = slice(c * D, (c + 1) * D)
        put_weight(
            "input", 3 * D // LANES, dot_tn(low_a[...], gp_s[:, at]), first_column=c * D
        )
    grad_normed = dot_nt(gp_s[...], w_in[...])
    put_vector("gain_a", column_sum(grad_normed * unit_a[...]))
    put_vector("shift_a", column_sum(grad_normed))
    grad_in = resid_s[...] + norm_back(grad_normed, unit_a[...], scale_a, vector("gain_a"))
    for b in range(slots):
        gin_ref[:, b, :] = grad_in[b * pad : b * pad + tokens, :].astype(LOW)


def block_pass(lay, full, images, upstream, counts):
    tokens, slots, _ = images.shape
    pad = -(-tokens // 16) * 16
    rows = slots * pad
    vmem = pl.BlockSpec(memory_space=pltpu.VMEM)
    flat = (lay.group * lay.padded, LANES)
    low = lambda *shape: pltpu.VMEM(shape, LOW)
    wide = lambda *shape: pltpu.VMEM(shape, F32)
    return pl.pallas_call(
        functools.partial(block_kernel, lay),
        out_shape=(
            jax.ShapeDtypeStruct(images.shape, LOW),
            jax.ShapeDtypeStruct(images.shape, LOW),
            jax.ShapeDtypeStruct(flat, F32),
        ),
        in_specs=[pl.BlockSpec(memory_space=pltpu.SMEM), vmem, vmem, vmem],
        out_specs=(vmem, vmem, vmem),
        scratch_shapes=[
            low(D, 3 * D), low(D, D), low(D, FF), low(FF, D), wide(FF, LANES),
            wide(rows, D), wide(rows, D), wide(rows, D), low(rows, D),
            low(rows, D), low(rows, D), low(rows, D),
            wide(slots * HEADS, pad, pad),
            low(rows, D), wide(rows, D), low(rows, D), low(rows, 3 * D), wide(rows, D),
        ],
        compiler_params=pltpu.CompilerParams(vmem_limit_bytes=40 * 2**20),
        name="block_pass",
    )(counts, full.reshape(flat), images, upstream)


def adamw_update(weights, first_moment, second_moment, gradient):
    first_new = 0.9 * first_moment + 0.1 * gradient
    second_new = 0.99 * second_moment + 0.01 * gradient * gradient
    first_hat = first_new / (1.0 - 0.9**STEP)
    second_hat = second_new / (1.0 - 0.99**STEP)
    weights_new = weights - 0.02 * (first_hat / (jnp.sqrt(second_hat) + 1e-08) + 0.05 * weights)
    return (weights_new, first_new, second_new)


def on_device(params, moment1, moment2, image_in, cotangent, image_counts):
    group, dp = lax.axis_size("group"), lax.axis_size("dp")
    lay = Layout(params.shape[0], group, dp)
    own = jnp.pad(params, (0, (lay.padded - lay.real) * LANES)).reshape(lay.padded, LANES)
    full = gather(lay, own)
    images, upstream = (jnp.swapaxes(v, 0, 1) for v in (image_in, cotangent))
    outputs, grad_inputs, grads = block_pass(lay, full, images, upstream, image_counts)
    outputs, grad_inputs = (jnp.swapaxes(v, 0, 1) for v in (outputs, grad_inputs))
    summed = reduce(lay, grads)
    count = image_in.shape[0] * group * dp
    grad_shard = summed.reshape(-1)[: params.shape[0]] * (1.0 / count)
    new_params, new_first, new_second = adamw_update(params, moment1, moment2, grad_shard)
    return (outputs, grad_inputs, grad_shard, new_params, new_first, new_second)


def solution(mesh):
    placed = (
        P("group"),
        P("group"),
        P("group"),
        P(("dp", "group"), None, None),
        P(("dp", "group"), None, None),
        P(("dp", "group")),
    )
    return jax.shard_map(
        on_device,
        mesh=mesh,
        in_specs=placed,
        out_specs=(
            P(("dp", "group"), None, None),
            P(("dp", "group"), None, None),
            P("group"),
            P("group"),
            P("group"),
            P("group"),
        ),
        check_vma=False,
    )
```
